32 devices in a mesh: row: 8 (over z, x), col: 4 (over y, core).
Axes of the slice: x: 2, y: 2, z: 4, core: 2. Of those that a mesh axis runs over, the one named last changes fastest.
Arguments:
- image_emb: bfloat16 [128, 4, 1024], P('row', 'col'), may hold values from -16 to 16
- text_emb: bfloat16 [64, 8, 1024], P('col', 'row'), may hold values from -16 to 16
- logit_scale: float32 [1], replicated, may hold values from 2.5 to 5
Outputs:
- loss: float32 [], replicated
- image_grad: float32 [128, 4, 1024], P('row', 'col')
- text_grad: float32 [64, 8, 1024], P('col', 'row')
The draws below stay inside these ranges and needn't reach their ends.
All inputs are finite; a program needn't handle non-finite values.
Results may differ from the reference program's by a relative error of at most 0.0075.
Values may be sent and summed in bfloat16 or wider, within the bound.
A program may use at most 64 MiB of HBM per device.

```python
import jax
import jax.numpy as jnp
from jax import lax

E = 1024
BLK = 16
N_ROW = 8
N_COL = 4


def draw_pairs(key):
    total_pairs = BLK * N_ROW * N_COL
    base_key = jax.random.fold_in(key, 7)
    shared = jax.random.truncated_normal(jax.random.fold_in(base_key, 1), -6.0, 6.0, (total_pairs, E), jnp.float32) / jnp.sqrt(1.0 * E)
    noise = jax.random.truncated_normal(jax.random.fold_in(base_key, 2), -6.0, 6.0, (total_pairs, E), jnp.float32) / jnp.sqrt(1.0 * E)
    rising = 1.0 + 2.0 * jnp.arange(total_pairs, dtype=jnp.float32)[:, None] / (total_pairs - 1)
    images = shared * rising
    texts = 0.6 * shared + 0.8 * noise
    return (images, texts)


def draw_image_emb(key, part):
    images, texts = draw_pairs(key)
    return images.reshape(BLK * N_ROW, N_COL, E).astype(jnp.bfloat16)


def draw_text_emb(key, part):
    images, texts = draw_pairs(key)
    return texts.reshape(BLK * N_COL, N_ROW, E).astype(jnp.bfloat16)


def setup_inputs(seed: int = 0) -> dict:
    arg_keys = jax.random.split(jax.random.key(seed), 4)
    image_emb = draw_image_emb(jax.random.fold_in(arg_keys[3], 71), 0)
    text_emb = draw_text_emb(jax.random.fold_in(arg_keys[3], 71), 0)
    logit_scale = jnp.clip(jax.random.uniform(arg_keys[2], (1,), jnp.float32, 2.5, 5.0), 2.5, 5.0)
    return {"image_emb": image_emb, "text_emb": text_emb, "logit_scale": logit_scale}


def reference(image_emb, text_emb, logit_scale):
    total_pairs = BLK * N_ROW * N_COL
    block_rows = BLK * N_COL
    images = image_emb.reshape(total_pairs, E)
    texts = text_emb.reshape(total_pairs, E)
    factor = logit_scale[0]
    image_blocks = images.reshape(N_ROW, block_rows, E)
    col_ids = jnp.arange(total_pairs, dtype=jnp.int32)

    def score_block(index, block):
        scores = factor * jnp.dot(block, texts.T, preferred_element_type=jnp.float32)
        row_ids = index * block_rows + jnp.arange(block_rows, dtype=jnp.int32)
        eye = row_ids[:, None] == col_ids[None, :]
        return scores, eye

    def first_pass(inputs):
        index, block = inputs
        scores, eye = score_block(index, block)
        peak = jnp.max(scores, axis=1)
        row_lse = peak + jnp.log(jnp.sum(jnp.exp(scores - peak[:, None]), axis=1))
        col_peak = jnp.max(scores, axis=0)
        col_sum = jnp.sum(jnp.exp(scores - col_peak[None, :]), axis=0)
        diag = jnp.sum(jnp.where(eye, scores, 0.0))
        return row_lse, col_peak, col_sum, diag

    indices = jnp.arange(N_ROW, dtype=jnp.int32)
    row_lse, col_peaks, col_sums, diags = lax.map(first_pass, (indices, image_blocks))
    overall = jnp.max(col_peaks, axis=0)
    col_lse = overall + jnp.log(jnp.sum(col_sums * jnp.exp(col_peaks - overall[None, :]), axis=0))
    loss = (jnp.sum(row_lse) + jnp.sum(col_lse) - 2.0 * jnp.sum(diags)) / (2.0 * total_pairs)

    def second_pass(carry, inputs):
        index, block, lse_rows = inputs
        scores, eye = score_block(index, block)
        delta = factor * (jnp.exp(scores - lse_rows[:, None]) + jnp.exp(scores - col_lse[None, :]) - 2.0 * eye.astype(jnp.float32))
        delta = delta.astype(jnp.bfloat16)
        grad_rows = jnp.dot(delta, texts, preferred_element_type=jnp.float32)
        carry = carry + jnp.dot(delta.T, block, preferred_element_type=jnp.float32)
        return carry, grad_rows

    start_text = jnp.zeros((total_pairs, E), jnp.float32)
    text_grad, image_rows = lax.scan(second_pass, start_text, (indices, image_blocks, row_lse))
    image_grad = image_rows.reshape(image_emb.shape)
    return loss, image_grad, text_grad.reshape(text_emb.shape)
```

```python
import functools

import jax
import jax.numpy as jnp
from jax import lax
from jax.experimental import pallas as pl
from jax.experimental.pallas import tpu as pltpu
from jax.sharding import PartitionSpec as P

MESH = pl.DeviceIdType.MESH
F32 = jnp.float32


def kernel(
    nr, nc, img_hbm, txt_hbm, scale,
    loss_ref, ig_ref, tg_ref,
    imgs, txts, rstat, cstat, iout, tout, iin, tin, iown, town, lrow, lcol,
    local_sem, send_sem, recv_sem,
):
    r = lax.axis_index("row")
    c = lax.axis_index("col")
    m, width = img_hbm.shape
    br, bc = m * nc, m * nr
    rows = [lax.rem(r + d, nr) for d in range(1, nr)]
    cols = [lax.rem(c + d, nc) for d in range(1, nc)]

    li = pltpu.make_async_copy(img_hbm, imgs.at[c], local_sem.at[0])
    lt = pltpu.make_async_copy(txt_hbm, txts.at[r], local_sem.at[1])
    li.start()
    lt.start()
    barrier = pltpu.get_barrier_semaphore()
    for p in rows:
        pl.semaphore_signal(barrier, inc=1, device_id=(p, c), device_id_type=MESH)
    for p in cols:
        pl.semaphore_signal(barrier, inc=1, device_id=(r, p), device_id_type=MESH)
    lt.wait()
    li.wait()
    pl.semaphore_wait(barrier, nr + nc - 2)

    def push(src, dst, k, dev):
        pltpu.make_async_remote_copy(
            src_ref=src, dst_ref=dst, send_sem=send_sem.at[k], recv_sem=recv_sem.at[k],
            device_id=dev, device_id_type=MESH,
        ).start()

    def arrived(ref, n, k):
        part = ref.at[pl.ds(0, n)]
        pltpu.make_async_copy(part, part, recv_sem.at[k]).wait()

    def left(ref, n, k):
        part = ref.at[pl.ds(0, n)]
        pltpu.make_async_copy(part, part, send_sem.at[k]).wait()

    for p in rows:
        push(txts.at[r], txts.at[r], 0, (p, c))
    for p in cols:
        push(imgs.at[c], imgs.at[c], 1, (r, p))
    factor = scale[0]
    arrived(imgs, nc - 1, 1)
    images = imgs[...].reshape(br, width)
    arrived(txts, nr - 1, 0)
    texts = txts[...].reshape(bc, width)
    s = factor * lax.dot_general(images, texts, (((1,), (1,)), ((), ())), preferred_element_type=F32)
    st = s.T

    def pair_i(i):
        return (r * m + lax.rem(i, m)) * nc + lax.div(i, m)

    def pair_t(i):
        return (c * m + lax.rem(i, m)) * nr + lax.div(i, m)

    eye = pair_i(lax.broadcasted_iota(jnp.int32, (br, bc), 0)) == pair_t(
        lax.broadcasted_iota(jnp.int32, (br, bc), 1)
    )
    eye_t = pair_t(lax.broadcasted_iota(jnp.int32, (bc, br), 0)) == pair_i(
        lax.broadcasted_iota(jnp.int32, (bc, br), 1)
    )

    cpeak = jnp.max(s, axis=0, keepdims=True)
    csum = jnp.sum(jnp.exp(s - cpeak), axis=0, keepdims=True)
    which = lax.broadcasted_iota(jnp.int32, (8, bc), 0)
    cstat[r] = jnp.where(which == 0, cpeak, csum)
    for p in rows:
        push(cstat.at[r], cstat.at[r], 2, (p, c))
    rpeak = jnp.max(st, axis=0, keepdims=True)
    rsum = jnp.sum(jnp.exp(st - rpeak), axis=0, keepdims=True)
    rdiag = jnp.sum(jnp.where(eye_t, st, 0.0), axis=0, keepdims=True)
    which = lax.broadcasted_iota(jnp.int32, (8, br), 0)
    rstat[c] = jnp.where(which == 0, rpeak, jnp.where(which == 1, rsum, rdiag))
    for p in cols:
        push(rstat.at[c], rstat.at[c], 3, (r, p))

    def lse(ref, n):
        peak = ref[0, 0:1, :]
        for k in range(1, n):
            peak = jnp.maximum(peak, ref[k, 0:1, :])
        total = jnp.zeros_like(peak)
        for k in range(n):
            total = total + ref[k, 1:2, :] * jnp.exp(ref[k, 0:1, :] - peak)
        return peak + jnp.log(total)

    arrived(rstat, nc - 1, 3)
    row_lse = lse(rstat, nc)
    diag = rstat[0, 2:3, :]
    for k in range(1, nc):
        diag = diag + rstat[k, 2:3, :]
    row_term = jnp.exp(s - jnp.broadcast_to(row_lse, (bc, br)).T) - jnp.where(eye, 2.0, 0.0)
    arrived(cstat, nr - 1, 2)
    col_lse = lse(cstat, nr)
    delta = factor * (row_term + jnp.exp(s - col_lse))
    delta_t = delta.T.astype(jnp.bfloat16)
    delta = delta.astype(jnp.bfloat16)

    tpart = jnp.dot(delta_t, images, preferred_element_type=F32).reshape(nr, m, width)
    town[...] = tpart
    tout[...] = tpart.astype(jnp.bfloat16)
    for d, p in enumerate(rows):
        push(tout.at[p], tin.at[d], 4, (p, c))
    ipart = jnp.dot(delta, texts, preferred_element_type=F32).reshape(nc, m, width)
    iown[...] = ipart
    iout[...] = ipart.astype(jnp.bfloat16)
    for d, p in enumerate(cols):
        push(iout.at[p], iin.at[d], 5, (r, p))

    lrow[r] = jnp.broadcast_to(jnp.sum(row_lse - 2.0 * diag, axis=1, keepdims=True), (8, 128))
    lcol[c] = jnp.broadcast_to(jnp.sum(col_lse, axis=1, keepdims=True), (8, 128))
    for p in rows:
        push(lrow.at[r], lrow.at[r], 6, (p, c))
    for p in cols:
        push(lcol.at[c], lcol.at[c], 7, (r, p))

    arrived(iin, nc - 1, 5)
    total = iown[c]
    for d in range(nc - 1):
        total = total + iin[d].astype(F32)
    ig_ref[...] = total
    arrived(tin, nr - 1, 4)
    total = town[r]
    for d in range(nr - 1):
        total = total + tin[d].astype(F32)
    tg_ref[...] = total
    arrived(lrow, nr - 1, 6)
    arrived(lcol, nc - 1, 7)
    total = lrow[0]
    for k in range(1, nr):
        total = total + lrow[k]
    for k in range(nc):
        total = total + lcol[k]
    loss_ref[0] = total[0, 0] / (2.0 * br * nr)

    left(txts, nr - 1, 0)
    left(imgs, nc - 1, 1)
    left(cstat, nr - 1, 2)
    left(rstat, nc - 1, 3)
    left(tin, nr - 1, 4)
    left(iin, nc - 1, 5)
    left(lrow, nr - 1, 6)
    left(lcol, nc - 1, 7)


def shards(nr, nc, image_emb, text_emb, logit_scale):
    m, _, width = image_emb.shape
    br, bc = m * nc, m * nr
    bf16 = jnp.bfloat16
    loss, ig, tg = pl.pallas_call(
        functools.partial(kernel, nr, nc),
        out_shape=(
            jax.ShapeDtypeStruct((1,), F32),
            jax.ShapeDtypeStruct((m, width), F32),
            jax.ShapeDtypeStruct((m, width), F32),
        ),
        in_specs=[
            pl.BlockSpec(memory_space=pl.ANY),
            pl.BlockSpec(memory_space=pl.ANY),
            pl.BlockSpec(memory_space=pltpu.SMEM),
        ],
        out_specs=(
            pl.BlockSpec(memory_space=pltpu.SMEM),
            pl.BlockSpec(memory_space=pltpu.VMEM),
            pl.BlockSpec(memory_space=pltpu.VMEM),
        ),
        scratch_shapes=[
            pltpu.VMEM((nc, m, width), bf16),
            pltpu.VMEM((nr, m, width), bf16),
            pltpu.VMEM((nc, 8, br), F32),
            pltpu.VMEM((nr, 8, bc), F32),
            pltpu.VMEM((nc, m, width), bf16),
            pltpu.VMEM((nr, m, width), bf16),
            pltpu.VMEM((nc - 1, m, width), bf16),
            pltpu.VMEM((nr - 1, m, width), bf16),
            pltpu.VMEM((nc, m, width), F32),
            pltpu.VMEM((nr, m, width), F32),
            pltpu.VMEM((nr, 8, 128), F32),
            pltpu.VMEM((nc, 8, 128), F32),
            pltpu.SemaphoreType.DMA((2,)),
            pltpu.SemaphoreType.DMA((8,)),
            pltpu.SemaphoreType.DMA((8,)),
        ],
        compiler_params=pltpu.CompilerParams(
            collective_id=0, has_side_effects=True, vmem_limit_bytes=40 * 1024 * 1024
        ),
    )(image_emb.reshape(m, width), text_emb.reshape(m, width), logit_scale)
    return loss[0], ig.reshape(m, 1, width), tg.reshape(m, 1, width)


def solution(mesh):
    return jax.shard_map(
        functools.partial(shards, mesh.shape["row"], mesh.shape["col"]),
        mesh=mesh,
        in_specs=(P("row", "col", None), P("col", "row", None), P()),
        out_specs=(P(), P("row", "col", None), P("col", "row", None)),
        check_vma=False,
    )
```

```python
import functools

import jax
import jax.numpy as jnp
from jax import lax
from jax.experimental import pallas as pl
from jax.experimental.pallas import tpu as pltpu
from jax.sharding import PartitionSpec as P

MESH = pl.DeviceIdType.MESH
F32 = jnp.float32


def kernel(
    nr, nc, lo, img_hbm, txt_hbm, scale,
    loss_ref, ig_ref, tg_ref,
    imgs, txts, rstat, cstat, iout, tout, iin, tin, iown, town, lrow, lcol,
    local_sem, send_sem, recv_sem,
):
    r = lax.axis_index("row")
    c = lax.axis_index("col")
    m, width = img_hbm.shape
    ni, nt = nr // lo, lo * nc
    br, bc = m * ni, m * nt
    hi_me, lo_me = lax.div(r, lo), lax.rem(r, lo)
    a, b = hi_me, lo_me * nc + c
    ipeers = [lax.rem(a + d, ni) for d in range(1, ni)]
    tpeers = [lax.rem(b + d, nt) for d in range(1, nt)]

    def idev(k):
        return (k * lo + lo_me, c)

    def tdev(q):
        return (hi_me * lo + lax.div(q, nc), lax.rem(q, nc))

    li = pltpu.make_async_copy(img_hbm, imgs.at[a], local_sem.at[0])
    lt = pltpu.make_async_copy(txt_hbm, txts.at[b], local_sem.at[1])
    li.start()
    lt.start()
    barrier = pltpu.get_barrier_semaphore()
    for p in tpeers:
        pl.semaphore_signal(barrier, inc=1, device_id=tdev(p), device_id_type=MESH)
    for p in ipeers:
        pl.semaphore_signal(barrier, inc=1, device_id=idev(p), device_id_type=MESH)
    lt.wait()
    li.wait()
    pl.semaphore_wait(barrier, ni + nt - 2)

    def push(src, dst, k, dev):
        pltpu.make_async_remote_copy(
            src_ref=src, dst_ref=dst, send_sem=send_sem.at[k], recv_sem=recv_sem.at[k],
            device_id=dev, device_id_type=MESH,
        ).start()

    def arrived(ref, n, k):
        part = ref.at[pl.ds(0, n)]
        pltpu.make_async_copy(part, part, recv_sem.at[k]).wait()

    def left(ref, n, k):
        part = ref.at[pl.ds(0, n)]
        pltpu.make_async_copy(part, part, send_sem.at[k]).wait()

    for p in tpeers:
        push(txts.at[b], txts.at[b], 0, tdev(p))
    for p in ipeers:
        push(imgs.at[a], imgs.at[a], 1, idev(p))
    factor = scale[0]
    arrived(imgs, ni - 1, 1)
    images = imgs[...].reshape(br, width)
    arrived(txts, nt - 1, 0)
    texts = txts[...].reshape(bc, width)
    s = factor * lax.dot_general(images, texts, (((1,), (1,)), ((), ())), preferred_element_type=F32)
    st = s.T

    def pair_i(i):
        return ((lax.div(i, m) * lo + lo_me) * m + lax.rem(i, m)) * nc + c

    def pair_t(i):
        q = lax.div(i, m)
        return (lax.rem(q, nc) * m + lax.rem(i, m)) * nr + hi_me * lo + lax.div(q, nc)

    eye = pair_i(lax.broadcasted_iota(jnp.int32, (br, bc), 0)) == pair_t(
        lax.broadcasted_iota(jnp.int32, (br, bc), 1)
    )
    eye_t = pair_t(lax.broadcasted_iota(jnp.int32, (bc, br), 0)) == pair_i(
        lax.broadcasted_iota(jnp.int32, (bc, br), 1)
    )

    cpeak = jnp.max(s, axis=0, keepdims=True)
    csum = jnp.sum(jnp.exp(s - cpeak), axis=0, keepdims=True)
    which = lax.broadcasted_iota(jnp.int32, (8, bc), 0)
    cstat[b] = jnp.where(which == 0, cpeak, csum)
    for p in tpeers:
        push(cstat.at[b], cstat.at[b], 2, tdev(p))
    rpeak = jnp.max(st, axis=0, keepdims=True)
    rsum = jnp.sum(jnp.exp(st - rpeak), axis=0, keepdims=True)
    rdiag = jnp.sum(jnp.where(eye_t, st, 0.0), axis=0, keepdims=True)
    which = lax.broadcasted_iota(jnp.int32, (8, br), 0)
    rstat[a] = jnp.where(which == 0, rpeak, jnp.where(which == 1, rsum, rdiag))
    for p in ipeers:
        push(rstat.at[a], rstat.at[a], 3, idev(p))

    def lse(ref, n):
        peak = ref[0, 0:1, :]
        for k in range(1, n):
            peak = jnp.maximum(peak, ref[k, 0:1, :])
        total = jnp.zeros_like(peak)
        for k in range(n):
            total = total + ref[k, 1:2, :] * jnp.exp(ref[k, 0:1, :] - peak)
        return peak + jnp.log(total)

    arrived(rstat, ni - 1, 3)
    row_lse = lse(rstat, ni)
    diag = rstat[0, 2:3, :]
    for k in range(1, ni):
        diag = diag + rstat[k, 2:3, :]
    row_term = jnp.exp(s - jnp.broadcast_to(row_lse, (bc, br)).T) - jnp.where(eye, 2.0, 0.0)
    arrived(cstat, nt - 1, 2)
    col_lse = lse(cstat, nt)
    delta = factor * (row_term + jnp.exp(s - col_lse))
    delta_t = delta.T.astype(jnp.bfloat16)
    delta = delta.astype(jnp.bfloat16)

    tpart = jnp.dot(delta_t, images, preferred_element_type=F32).reshape(nt, m, width)
    town[...] = tpart
    tout[...] = tpart.astype(jnp.bfloat16)
    for d, p in enumerate(tpeers):
        push(tout.at[p], tin.at[d], 4, tdev(p))
    ipart = jnp.dot(delta, texts, preferred_element_type=F32).reshape(ni, m, width)
    iown[...] = ipart
    iout[...] = ipart.astype(jnp.bfloat16)
    for d, p in enumerate(ipeers):
        push(iout.at[p], iin.at[d], 5, idev(p))

    lrow[b] = jnp.broadcast_to(jnp.sum(row_lse - 2.0 * diag, axis=1, keepdims=True), (8, 128))
    lcol[a] = jnp.broadcast_to(jnp.sum(col_lse, axis=1, keepdims=True), (8, 128))
    for p in tpeers:
        push(lrow.at[b], lrow.at[b], 6, tdev(p))
    for p in ipeers:
        push(lcol.at[a], lcol.at[a], 7, idev(p))

    arrived(iin, ni - 1, 5)
    total = iown[a]
    for d in range(ni - 1):
        total = total + iin[d].astype(F32)
    ig_ref[...] = total
    arrived(tin, nt - 1, 4)
    total = town[b]
    for d in range(nt - 1):
        total = total + tin[d].astype(F32)
    tg_ref[...] = total
    arrived(lrow, nt - 1, 6)
    arrived(lcol, ni - 1, 7)
    total = lrow[0]
    for k in range(1, nt):
        total = total + lrow[k]
    for k in range(ni):
        total = total + lcol[k]
    loss_ref[0] = total[0, 0] / (2.0 * m * nr * nc)

    left(txts, nt - 1, 0)
    left(imgs, ni - 1, 1)
    left(cstat, nt - 1, 2)
    left(rstat, ni - 1, 3)
    left(tin, nt - 1, 4)
    left(iin, ni - 1, 5)
    left(lrow, nt - 1, 6)
    left(lcol, ni - 1, 7)


def shards(nr, nc, image_emb, text_emb, logit_scale):
    m, _, width = image_emb.shape
    lo = 2 if nr % 2 == 0 else 1
    ni, nt = nr // lo, lo * nc
    br, bc = m * ni, m * nt
    bf16 = jnp.bfloat16
    loss, ig, tg = pl.pallas_call(
        functools.partial(kernel, nr, nc, lo),
        out_shape=(
            jax.ShapeDtypeStruct((1,), F32),
            jax.ShapeDtypeStruct((m, width), F32),
            jax.ShapeDtypeStruct((m, width), F32),
        ),
        in_specs=[
            pl.BlockSpec(memory_space=pltpu.HBM),
            pl.BlockSpec(memory_space=pltpu.HBM),
            pl.BlockSpec(memory_space=pltpu.SMEM),
        ],
        out_specs=(
            pl.BlockSpec(memory_space=pltpu.SMEM),
            pl.BlockSpec(memory_space=pltpu.VMEM),
            pl.BlockSpec(memory_space=pltpu.VMEM),
        ),
        scratch_shapes=[
            pltpu.VMEM((ni, m, width), bf16),
            pltpu.VMEM((nt, m, width), bf16),
            pltpu.VMEM((ni, 8, br), F32),
            pltpu.VMEM((nt, 8, bc), F32),
            pltpu.VMEM((ni, m, width), bf16),
            pltpu.VMEM((nt, m, width), bf16),
            pltpu.VMEM((ni - 1, m, width), bf16),
            pltpu.VMEM((nt - 1, m, width), bf16),
            pltpu.VMEM((ni, m, width), F32),
            pltpu.VMEM((nt, m, width), F32),
            pltpu.VMEM((nt, 8, 128), F32),
            pltpu.VMEM((ni, 8, 128), F32),
            pltpu.SemaphoreType.DMA((2,)),
            pltpu.SemaphoreType.DMA((8,)),
            pltpu.SemaphoreType.DMA((8,)),
        ],
        compiler_params=pltpu.CompilerParams(
            collective_id=0, has_side_effects=True, vmem_limit_bytes=40 * 1024 * 1024
        ),
    )(image_emb.reshape(m, width), text_emb.reshape(m, width), logit_scale)
    return loss[0], ig.reshape(m, 1, width), tg.reshape(m, 1, width)


def solution(mesh):
    return jax.shard_map(
        functools.partial(shards, mesh.shape["row"], mesh.shape["col"]),
        mesh=mesh,
        in_specs=(P("row", "col", None), P("col", "row", None), P()),
        out_specs=(P(), P("row", "col", None), P("col", "row", None)),
        check_vma=False,
    )
```

```python
import functools

import jax
import jax.numpy as jnp
from jax import lax
from jax.experimental import pallas as pl
from jax.experimental.pallas import tpu as pltpu
from jax.sharding import PartitionSpec as P

MESH = pl.DeviceIdType.MESH
F32 = jnp.float32


def kernel(
    nr, nc, lo, img_hbm, txt_hbm, scale,
    loss_ref, ig_ref, tg_ref,
    imgs, txts, rstat, cstat, iout, tout, iin, tin, idelta, tdelta, lrow, lcol,
    local_sem, send_sem, recv_sem,
):
    r = lax.axis_index("row")
    c = lax.axis_index("col")
    m, width = img_hbm.shape
    ni, nt = nr // lo, lo * nc
    br, bc = m * ni, m * nt
    hi_me, lo_me = lax.div(r, lo), lax.rem(r, lo)
    a, b = hi_me, lo_me * nc + c
    ipeers = [lax.rem(a + d, ni) for d in range(1, ni)]
    tpeers = [lax.rem(b + d, nt) for d in range(1, nt)]

    def idev(k):
        return (k * lo + lo_me, c)

    def tdev(q):
        return (hi_me * lo + lax.div(q, nc), lax.rem(q, nc))

    li = pltpu.make_async_copy(img_hbm, imgs.at[a], local_sem.at[0])
    lt = pltpu.make_async_copy(txt_hbm, txts.at[b], local_sem.at[1])
    li.start()
    lt.start()
    barrier = pltpu.get_barrier_semaphore()
    for p in tpeers:
        pl.semaphore_signal(barrier, inc=1, device_id=tdev(p), device_id_type=MESH)
    for p in ipeers:
        pl.semaphore_signal(barrier, inc=1, device_id=idev(p), device_id_type=MESH)
    pl.semaphore_wait(barrier, ni + nt - 2)

    def push(src, dst, k, dev):
        pltpu.make_async_remote_copy(
            src_ref=src, dst_ref=dst, send_sem=send_sem.at[k], recv_sem=recv_sem.at[k],
            device_id=dev, device_id_type=MESH,
        ).start()

    def arrived(ref, n, k):
        part = ref.at[pl.ds(0, n)]
        pltpu.make_async_copy(part, part, recv_sem.at[k]).wait()

    def left(ref, n, k):
        part = ref.at[pl.ds(0, n)]
        pltpu.make_async_copy(part, part, send_sem.at[k]).wait()

    for p in tpeers:
        push(txt_hbm, txts.at[b], 0, tdev(p))
    for p in ipeers:
        push(img_hbm, imgs.at[a], 1, idev(p))
    factor = scale[0]
    li.wait()
    lt.wait()
    arrived(imgs, ni - 1, 1)
    images = imgs[...].reshape(br, width)
    arrived(txts, nt - 1, 0)
    texts = txts[...].reshape(bc, width)
    s = factor * lax.dot_general(images, texts, (((1,), (1,)), ((), ())), preferred_element_type=F32)
    st = s.T

    def pair_i(i):
        return ((lax.div(i, m) * lo + lo_me) * m + lax.rem(i, m)) * nc + c

    def pair_t(i):
        q = lax.div(i, m)
        return (lax.rem(q, nc) * m + lax.rem(i, m)) * nr + hi_me * lo + lax.div(q, nc)

    eye_t = pair_t(lax.broadcasted_iota(jnp.int32, (bc, br), 0)) == pair_i(
        lax.broadcasted_iota(jnp.int32, (bc, br), 1)
    )

    cpeak = jnp.max(s, axis=0, keepdims=True)
    cexp = jnp.exp(s - cpeak)
    csum = jnp.sum(cexp, axis=0, keepdims=True)
    which = lax.broadcasted_iota(jnp.int32, (8, bc), 0)
    cstat[b] = jnp.where(which == 0, cpeak, csum)
    for p in tpeers:
        push(cstat.at[b], cstat.at[b], 2, tdev(p))
    rpeak = jnp.max(st, axis=0, keepdims=True)
    rexp = jnp.exp(st - rpeak)
    rsum = jnp.sum(rexp, axis=0, keepdims=True)
    rdiag = jnp.sum(jnp.where(eye_t, st, 0.0), axis=0, keepdims=True)
    which = lax.broadcasted_iota(jnp.int32, (8, br), 0)
    rstat[a] = jnp.where(which == 0, rpeak, jnp.where(which == 1, rsum, rdiag))
    for p in ipeers:
        push(rstat.at[a], rstat.at[a], 3, idev(p))

    def lse(ref, n):
        peak = ref[0, 0:1, :]
        for k in range(1, n):
            peak = jnp.maximum(peak, ref[k, 0:1, :])
        total = jnp.zeros_like(peak)
        for k in range(n):
            total = total + ref[k, 1:2, :] * jnp.exp(ref[k, 0:1, :] - peak)
        return peak + jnp.log(total)

    arrived(rstat, ni - 1, 3)
    row_lse = lse(rstat, ni)
    diag = rstat[0, 2:3, :]
    for k in range(1, ni):
        diag = diag + rstat[k, 2:3, :]
    row_term = factor * (rexp * jnp.exp(rpeak - row_lse) - jnp.where(eye_t, 2.0, 0.0))
    arrived(cstat, nt - 1, 2)
    col_lse = lse(cstat, nt)
    col_term = factor * (cexp * jnp.exp(cpeak - col_lse))
    delta = (row_term.T + col_term).astype(jnp.bfloat16)
    delta_t = (row_term + col_term.T).astype(jnp.bfloat16)

    ipart = jnp.dot(delta, texts, preferred_element_type=F32)
    iout[...] = ipart.astype(jnp.bfloat16).reshape(ni, m, width)
    for d, p in enumerate(ipeers):
        push(iout.at[p], iin.at[d], 5, idev(p))
    tpart = jnp.dot(delta_t, images, preferred_element_type=F32)
    tout[...] = tpart.astype(jnp.bfloat16).reshape(nt, m, width)
    for d, p in enumerate(tpeers):
        push(tout.at[p], tin.at[d], 4, tdev(p))

    idelta[...] = delta.reshape(ni, m, bc)
    tdelta[...] = delta_t.reshape(nt, m, br)
    lrow[b] = jnp.broadcast_to(jnp.sum(row_lse - 2.0 * diag, axis=1, keepdims=True), (8, 128))
    lcol[a] = jnp.broadcast_to(jnp.sum(col_lse, axis=1, keepdims=True), (8, 128))
    for p in tpeers:
        push(lrow.at[b], lrow.at[b], 6, tdev(p))
    for p in ipeers:
        push(lcol.at[a], lcol.at[a], 7, idev(p))

    image_total = jnp.dot(idelta[a], texts, preferred_element_type=F32)
    text_total = jnp.dot(tdelta[b], images, preferred_element_type=F32)
    arrived(iin, ni - 1, 5)
    for d in range(ni - 1):
        image_total = image_total + iin[d].astype(F32)
    ig_ref[...] = image_total
    arrived(tin, nt - 1, 4)
    for d in range(nt - 1):
        text_total = text_total + tin[d].astype(F32)
    tg_ref[...] = text_total
    arrived(lrow, nt - 1, 6)
    arrived(lcol, ni - 1, 7)
    total = lrow[0]
    for k in range(1, nt):
        total = total + lrow[k]
    for k in range(ni):
        total = total + lcol[k]
    loss_ref[0] = total[0, 0] / (2.0 * m * nr * nc)

    left(txts, nt - 1, 0)
    left(imgs, ni - 1, 1)
    left(cstat, nt - 1, 2)
    left(rstat, ni - 1, 3)
    left(tin, nt - 1, 4)
    left(iin, ni - 1, 5)
    left(lrow, nt - 1, 6)
    left(lcol, ni - 1, 7)


def shards(nr, nc, image_emb, text_emb, logit_scale):
    m, _, width = image_emb.shape
    lo = 2 if nr % 2 == 0 else 1
    ni, nt = nr // lo, lo * nc
    br, bc = m * ni, m * nt
    bf16 = jnp.bfloat16
    loss, ig, tg = pl.pallas_call(
        functools.partial(kernel, nr, nc, lo),
        out_shape=(
            jax.ShapeDtypeStruct((1,), F32),
            jax.ShapeDtypeStruct((m, width), F32),
            jax.ShapeDtypeStruct((m, width), F32),
        ),
        in_specs=[
            pl.BlockSpec(memory_space=pltpu.HBM),
            pl.BlockSpec(memory_space=pltpu.HBM),
            pl.BlockSpec(memory_space=pltpu.SMEM),
        ],
        out_specs=(
            pl.BlockSpec(memory_space=pltpu.SMEM),
            pl.BlockSpec(memory_space=pltpu.VMEM),
            pl.BlockSpec(memory_space=pltpu.VMEM),
        ),
        scratch_shapes=[
            pltpu.VMEM((ni, m, width), bf16),
            pltpu.VMEM((nt, m, width), bf16),
            pltpu.VMEM((ni, 8, br), F32),
            pltpu.VMEM((nt, 8, bc), F32),
            pltpu.VMEM((ni, m, width), bf16),
            pltpu.VMEM((nt, m, width), bf16),
            pltpu.VMEM((ni - 1, m, width), bf16),
            pltpu.VMEM((nt - 1, m, width), bf16),
            pltpu.VMEM((ni, m, bc), bf16),
            pltpu.VMEM((nt, m, br), bf16),
            pltpu.VMEM((nt, 8, 128), F32),
            pltpu.VMEM((ni, 8, 128), F32),
            pltpu.SemaphoreType.DMA((2,)),
            pltpu.SemaphoreType.DMA((8,)),
            pltpu.SemaphoreType.DMA((8,)),
        ],
        compiler_params=pltpu.CompilerParams(
            collective_id=0, has_side_effects=True, vmem_limit_bytes=40 * 1024 * 1024
        ),
    )(
        pltpu.with_memory_space_constraint(image_emb.reshape(m, width), pltpu.HBM),
        pltpu.with_memory_space_constraint(text_emb.reshape(m, width), pltpu.HBM),
        logit_scale,
    )
    return loss[0], ig.reshape(m, 1, width), tg.reshape(m, 1, width)


def solution(mesh):
    return jax.shard_map(
        functools.partial(shards, mesh.shape["row"], mesh.shape["col"]),
        mesh=mesh,
        in_specs=(P("row", "col", None), P("col", "row", None), P()),
        out_specs=(P(), P("row", "col", None), P("col", "row", None)),
        check_vma=False,
    )
```

```python
import functools

import jax
import jax.numpy as jnp
from jax import lax
from jax.experimental import pallas as pl
from jax.experimental.pallas import tpu as pltpu
from jax.sharding import PartitionSpec as P

MESH = pl.DeviceIdType.MESH
F32 = jnp.float32


def kernel(
    nr, nc, lo, img_hbm, txt_hbm, scale,
    loss_ref, ig_ref, tg_ref,
    imgs, txts, rstat, cstat, iout, tout, iin, tin, idelta, tdelta, lrow, lcol,
    local_sem, send_sem, recv_sem,
):
    r = lax.axis_index("row")
    c = lax.axis_index("col")
    m, width = img_hbm.shape
    ni, nt = nr // lo, lo * nc
    br, bc = m * ni, m * nt
    hi_me, lo_me = lax.div(r, lo), lax.rem(r, lo)
    a, b = hi_me, lo_me * nc + c
    ipeers = [lax.rem(a + d, ni) for d in range(1, ni)]
    tpeers = [lax.rem(b + d, nt) for d in range(1, nt)]

    def idev(k):
        return (k * lo + lo_me, c)

    def tdev(q):
        return (hi_me * lo + lax.div(q, nc), lax.rem(q, nc))

    li = pltpu.make_async_copy(img_hbm, imgs.at[a], local_sem.at[0])
    lt = pltpu.make_async_copy(txt_hbm, txts.at[b], local_sem.at[1])
    li.start()
    lt.start()
    barrier = pltpu.get_barrier_semaphore()
    for p in tpeers:
        pl.semaphore_signal(barrier, inc=1, device_id=tdev(p), device_id_type=MESH)
    for p in ipeers:
        pl.semaphore_signal(barrier, inc=1, device_id=idev(p), device_id_type=MESH)
    pl.semaphore_wait(barrier, ni + nt - 2)

    def push(src, dst, k, dev):
        pltpu.make_async_remote_copy(
            src_ref=src, dst_ref=dst, send_sem=send_sem.at[k], recv_sem=recv_sem.at[k],
            device_id=dev, device_id_type=MESH,
        ).start()

    def arrived(ref, n, k):
        part = ref.at[pl.ds(0, n)]
        pltpu.make_async_copy(part, part, recv_sem.at[k]).wait()

    def left(ref, n, k):
        part = ref.at[pl.ds(0, n)]
        pltpu.make_async_copy(part, part, send_sem.at[k]).wait()

    for p in tpeers:
        push(txt_hbm, txts.at[b], 0, tdev(p))
    for p in ipeers:
        push(img_hbm, imgs.at[a], 1, idev(p))
    factor = scale[0]
    li.wait()
    lt.wait()
    arrived(imgs, ni - 1, 1)
    images = imgs[...].reshape(br, width)
    arrived(txts, nt - 1, 0)
    texts = txts[...].reshape(bc, width)
    s = factor * lax.dot_general(images, texts, (((1,), (1,)), ((), ())), preferred_element_type=F32)
    st = s.T

    def pair_i(i):
        return ((lax.div(i, m) * lo + lo_me) * m + lax.rem(i, m)) * nc + c

    def pair_t(i):
        q = lax.div(i, m)
        return (lax.rem(q, nc) * m + lax.rem(i, m)) * nr + hi_me * lo + lax.div(q, nc)

    eye_t = pair_t(lax.broadcasted_iota(jnp.int32, (bc, br), 0)) == pair_i(
        lax.broadcasted_iota(jnp.int32, (bc, br), 1)
    )

    cpeak = jnp.max(s, axis=0, keepdims=True)
    cexp = jnp.exp(s - cpeak)
    csum = jnp.sum(cexp, axis=0, keepdims=True)
    which = lax.broadcasted_iota(jnp.int32, (8, bc), 0)
    cstat[b] = jnp.where(which == 0, cpeak, csum)
    for p in tpeers:
        push(cstat.at[b], cstat.at[b], 2, tdev(p))
    rpeak = jnp.max(st, axis=0, keepdims=True)
    rexp = jnp.exp(st - rpeak)
    rsum = jnp.sum(rexp, axis=0, keepdims=True)
    rdiag = jnp.sum(jnp.where(eye_t, st, 0.0), axis=0, keepdims=True)
    which = lax.broadcasted_iota(jnp.int32, (8, br), 0)
    rstat[a] = jnp.where(which == 0, rpeak, jnp.where(which == 1, rsum, rdiag))
    for p in ipeers:
        push(rstat.at[a], rstat.at[a], 3, idev(p))

    def lse(ref, n):
        peak = ref[0, 0:1, :]
        for k in range(1, n):
            peak = jnp.maximum(peak, ref[k, 0:1, :])
        total = jnp.zeros_like(peak)
        for k in range(n):
            total = total + ref[k, 1:2, :] * jnp.exp(ref[k, 0:1, :] - peak)
        return peak + jnp.log(total)

    arrived(rstat, ni - 1, 3)
    row_lse = lse(rstat, ni)
    diag = rstat[0, 2:3, :]
    for k in range(1, ni):
        diag = diag + rstat[k, 2:3, :]
    row_term = factor * (rexp * jnp.exp(rpeak - row_lse) - jnp.where(eye_t, 2.0, 0.0))
    arrived(cstat, nt - 1, 2)
    col_lse = lse(cstat, nt)
    lrow[b] = jnp.broadcast_to(jnp.sum(row_lse - 2.0 * diag, axis=1, keepdims=True), (8, 128))
    lcol[a] = jnp.broadcast_to(jnp.sum(col_lse, axis=1, keepdims=True), (8, 128))
    for p in tpeers:
        push(lrow.at[b], lrow.at[b], 6, tdev(p))
    for p in ipeers:
        push(lcol.at[a], lcol.at[a], 7, idev(p))
    col_term = factor * (cexp * jnp.exp(cpeak - col_lse))
    delta = (row_term.T + col_term).astype(jnp.bfloat16)
    delta_t = (row_term + col_term.T).astype(jnp.bfloat16)

    ipart = jnp.dot(delta, texts, preferred_element_type=F32)
    iout[...] = ipart.astype(jnp.bfloat16).reshape(ni, m, width)
    for d, p in enumerate(ipeers):
        push(iout.at[p], iin.at[d], 5, idev(p))
    tpart = jnp.dot(delta_t, images, preferred_element_type=F32)
    tout[...] = tpart.astype(jnp.bfloat16).reshape(nt, m, width)
    for d, p in enumerate(tpeers):
        push(tout.at[p], tin.at[d], 4, tdev(p))

    idelta[...] = delta.reshape(ni, m, bc)
    tdelta[...] = delta_t.reshape(nt, m, br)
    image_total = jnp.dot(idelta[a], texts, preferred_element_type=F32)
    text_total = jnp.dot(tdelta[b], images, preferred_element_type=F32)
    arrived(iin, ni - 1, 5)
    for d in range(ni - 1):
        image_total = image_total + iin[d].astype(F32)
    ig_ref[...] = image_total
    arrived(tin, nt - 1, 4)
    for d in range(nt - 1):
        text_total = text_total + tin[d].astype(F32)
    tg_ref[...] = text_total
    arrived(lrow, nt - 1, 6)
    arrived(lcol, ni - 1, 7)
    total = lrow[0]
    for k in range(1, nt):
        total = total + lrow[k]
    for k in range(ni):
        total = total + lcol[k]
    loss_ref[0] = total[0, 0] / (2.0 * m * nr * nc)

    left(txts, nt - 1, 0)
    left(imgs, ni - 1, 1)
    left(cstat, nt - 1, 2)
    left(rstat, ni - 1, 3)
    left(tin, nt - 1, 4)
    left(iin, ni - 1, 5)
    left(lrow, nt - 1, 6)
    left(lcol, ni - 1, 7)


def shards(nr, nc, image_emb, text_emb, logit_scale):
    m, _, width = image_emb.shape
    lo = 2 if nr % 2 == 0 else 1
    ni, nt = nr // lo, lo * nc
    br, bc = m * ni, m * nt
    bf16 = jnp.bfloat16
    loss, ig, tg = pl.pallas_call(
        functools.partial(kernel, nr, nc, lo),
        out_shape=(
            jax.ShapeDtypeStruct((1,), F32),
            jax.ShapeDtypeStruct((m, width), F32),
            jax.ShapeDtypeStruct((m, width), F32),
        ),
        in_specs=[
            pl.BlockSpec(memory_space=pltpu.HBM),
            pl.BlockSpec(memory_space=pltpu.HBM),
            pl.BlockSpec(memory_space=pltpu.SMEM),
        ],
        out_specs=(
            pl.BlockSpec(memory_space=pltpu.SMEM),
            pl.BlockSpec(memory_space=pltpu.VMEM),
            pl.BlockSpec(memory_space=pltpu.VMEM),
        ),
        scratch_shapes=[
            pltpu.VMEM((ni, m, width), bf16),
            pltpu.VMEM((nt, m, width), bf16),
            pltpu.VMEM((ni, 8, br), F32),
            pltpu.VMEM((nt, 8, bc), F32),
            pltpu.VMEM((ni, m, width), bf16),
            pltpu.VMEM((nt, m, width), bf16),
            pltpu.VMEM((ni - 1, m, width), bf16),
            pltpu.VMEM((nt - 1, m, width), bf16),
            pltpu.VMEM((ni, m, bc), bf16),
            pltpu.VMEM((nt, m, br), bf16),
            pltpu.VMEM((nt, 8, 128), F32),
            pltpu.VMEM((ni, 8, 128), F32),
            pltpu.SemaphoreType.DMA((2,)),
            pltpu.SemaphoreType.DMA((8,)),
            pltpu.SemaphoreType.DMA((8,)),
        ],
        compiler_params=pltpu.CompilerParams(
            collective_id=0, has_side_effects=True, vmem_limit_bytes=40 * 1024 * 1024
        ),
    )(
        pltpu.with_memory_space_constraint(image_emb.reshape(m, width), pltpu.HBM),
        pltpu.with_memory_space_constraint(text_emb.reshape(m, width), pltpu.HBM),
        logit_scale,
    )
    return loss[0], ig.reshape(m, 1, width), tg.reshape(m, 1, width)


def solution(mesh):
    return jax.shard_map(
        functools.partial(shards, mesh.shape["row"], mesh.shape["col"]),
        mesh=mesh,
        in_specs=(P("row", "col", None), P("col", "row", None), P()),
        out_specs=(P(), P("row", "col", None), P("col", "row", None)),
        check_vma=False,
    )
```
